32 devices in a mesh: grp: 2 (over x), tm: 16 (over z, y, core).
Axes of the slice: x: 2, y: 2, z: 4, core: 2. Of those that a mesh axis runs over, the one named last changes fastest.
Arguments:
- noise: float32 [32, 256, 256], P(('grp', 'tm')), parts along dimension 0, may hold values from -6 to 6
- phonon_level: int32 [32, 256, 256], P(('grp', 'tm')), parts along dimension 0, may hold values from 0 to 16
- hop_x: float32 [256, 256], replicated, as said below
- hop_y: float32 [256, 256], replicated, as said below
Outputs:
- solution: float32 [32, 256, 256], P(('grp', 'tm')), parts along dimension 0
- residual: float32 [32, 256, 256], P(('grp', 'tm')), parts along dimension 0
The draws below stay inside these ranges and needn't reach their ends.
There are 2 independent parts, one for each index of `grp`. The reference program is written for one: setup_inputs(seed, part) draws one part's arguments, and reference() takes and returns one part's arrays. A program takes and returns all parts, laid end to end along the dimension named above; an argument that names none is the same for every part. Nothing has to cross between parts.
Inputs may be any that keep to these rules, and one draw needn't show every extreme that they name: hop_x is symmetric. hop_y is symmetric.
All inputs are finite; a program needn't handle non-finite values.
Results may differ from the reference program's by a relative error of at most 0.0003.
Values sent between devices are 32-bit elements; how exact they have to be, the bound alone decides.
A program may use at most 64 MiB of HBM per device.

```python
import math
import jax
import jax.numpy as jnp
from jax import lax

LX = 256
LY = 256
ORDER = 10
LEVELS = 17
L = 16


def draw_phonon_level(key, part):
    times = jnp.arange(L, dtype=jnp.int32)
    offset = (LEVELS - 9) * times // (L - 1)
    levels = jax.random.randint(key, (L, LX, LY), 0, 9, dtype=jnp.int32) + offset[:, None, None]
    levels = levels.at[0, 0, 0].set(0)
    levels = levels.at[L - 1, 0, 0].set(LEVELS - 1)
    return levels


def hop_matrix(key, length):
    noise_part = jax.random.normal(key, (length, length), jnp.float32)
    noise_part = noise_part * (0.25 / math.sqrt(length))
    return jnp.eye(length, dtype=jnp.float32) + (noise_part + noise_part.T) * 0.70710678


def draw_hop_x(key, part):
    return hop_matrix(jax.random.fold_in(key, 11), LX)


def draw_hop_y(key, part):
    return hop_matrix(jax.random.fold_in(key, 12), LY)


def block_levels(own_key, shape, split, smallest, largest):
    def one(dim, blocks):
        steps = jax.random.uniform(jax.random.fold_in(jax.random.fold_in(own_key, 6), dim), (blocks,), jnp.float32, smallest / len(split), largest / len(split))
        return jnp.repeat(jnp.exp(steps), shape[dim] // blocks).reshape((-1,) + (1,) * (len(shape) - dim - 1))

    loudness = one(*split[0])
    for cut in split[1:]:
        loudness = loudness * one(*cut)
    return loudness


def bell_draw(key, shape, scale, bound, shards=(), kind=jnp.bfloat16):
    loudness = block_levels(key, shape, shards, -0.22, 0.18) if shards else 1.0
    values = jax.random.normal(key, shape, jnp.float32) * scale * loudness
    return jnp.minimum(jnp.maximum(values, -bound), bound).astype(kind)


def setup_inputs(seed: int = 0, part: int = 0) -> dict:
    splits = jax.random.split(jax.random.key(seed), 5)
    own_keys = jax.random.split(jax.random.fold_in(splits[4], part), 5)
    noise = bell_draw(own_keys[0], (L, LX, LY), 1.0, 6.0, ((0, 16),), jnp.float32)
    phonon_level = draw_phonon_level(jax.random.fold_in(jax.random.fold_in(splits[4], part), 71), part)
    hop_x = draw_hop_x(jax.random.fold_in(splits[4], 71), part)
    hop_y = draw_hop_y(jax.random.fold_in(splits[4], 71), part)
    return {"noise": noise, "phonon_level": phonon_level, "hop_x": hop_x, "hop_y": hop_y}


def propagate(field, hop_x, hop_y):
    inner = jnp.einsum('ax,nxy->nay', hop_x, field, precision=lax.Precision.HIGHEST)
    return jnp.einsum('nay,yb->nab', inner, hop_y, precision=lax.Precision.HIGHEST)

def normal_apply(vector, damp, hop_x, hop_y):
    length = vector.shape[0]
    positions = jnp.arange(length, dtype=jnp.int32)
    first_sign = jnp.where(positions == 0, -1.0, 1.0).astype(jnp.float32)[:, None, None]
    last_sign = jnp.where(positions == length - 1, -1.0, 1.0).astype(jnp.float32)[:, None, None]
    previous = jnp.roll(vector, 1, axis=0) * first_sign
    forward = vector - propagate(damp * previous, hop_x, hop_y)
    carried = damp * propagate(forward, hop_x, hop_y)
    following = jnp.roll(carried, -1, axis=0) * last_sign
    return forward - following

def chebyshev(field, cosines, cbar, hop_x, hop_y):
    lower_edge = 0.05
    upper_edge = (1.0 + 3.0 * cbar) ** 2
    center = (upper_edge + lower_edge) / (upper_edge - lower_edge)
    radius_term = jnp.sqrt(center * center - 1.0)
    ratio = center - radius_term
    cos_block = cosines[:, None, None]

    def apply_shifted(vector):
        once = propagate(vector, hop_x, hop_y)
        twice = propagate(once, hop_x, hop_y)
        normal_part = vector + cbar * cbar * twice - 2.0 * cbar * cos_block * once
        return (2.0 * normal_part - (upper_edge + lower_edge) * vector) / (upper_edge - lower_edge)
    previous = field
    current = apply_shifted(field)
    weight = -ratio
    total_sum = previous + 2.0 * weight * current
    for degree in range(2, ORDER + 1):
        following = 2.0 * apply_shifted(current) - previous
        weight = weight * -ratio
        total_sum = total_sum + 2.0 * weight * following
        previous = current
        current = following
    return total_sum * (2.0 / ((upper_edge - lower_edge) * radius_term))

def precondition(resid, cbar, hop_x, hop_y):
    length = resid.shape[0]
    times = jnp.arange(length, dtype=jnp.int32)
    phase = (2 * times[:, None] + 1) * times[None, :] % (2 * length)
    angles = phase.astype(jnp.float32) * (math.pi / length)
    cos_table = jnp.cos(angles)
    sin_table = jnp.sin(angles)
    flat = resid.reshape(length, -1)
    real_part = jnp.dot(cos_table, flat, precision=lax.Precision.HIGHEST)
    imag_part = -jnp.dot(sin_table, flat, precision=lax.Precision.HIGHEST)
    cosines = jnp.cos((2 * times + 1).astype(jnp.float32) * (math.pi / length))
    stacked = jnp.concatenate([real_part, imag_part], axis=0).reshape(2 * length, resid.shape[1], resid.shape[2])
    result = chebyshev(stacked, jnp.concatenate([cosines, cosines]), cbar, hop_x, hop_y)
    result = result.reshape(2 * length, -1)
    back = jnp.dot(cos_table.T, result[:length], precision=lax.Precision.HIGHEST) - jnp.dot(sin_table.T, result[length:], precision=lax.Precision.HIGHEST)
    return (back / length).reshape(resid.shape)

def reference(noise, phonon_level, hop_x, hop_y):
    middle = (LEVELS - 1) // 2
    levels = phonon_level.astype(jnp.float32)
    damp = jnp.exp(-0.05 * (levels - middle))
    mean_level = jnp.sum(levels) / (L * LX * LY)
    cbar = jnp.exp(-0.05 * (mean_level - middle))
    first = precondition(noise, cbar, hop_x, hop_y)
    second_residual = noise - normal_apply(first, damp, hop_x, hop_y)
    solution = first + precondition(second_residual, cbar, hop_x, hop_y)
    residual = noise - normal_apply(solution, damp, hop_x, hop_y)
    return (solution, residual)
```

```python
import functools
import math

import jax
import jax.numpy as jnp
from jax import lax
from jax.experimental import pallas as pl
from jax.experimental.pallas import tpu as pltpu
from jax.sharding import PartitionSpec as P

ORDER = 10
LEVELS = 17


def from_behind(value, axis, steps):
    count = lax.axis_size(axis)
    pairs = [(source, (source + steps) % count) for source in range(count)]
    return lax.ppermute(value, axis, pairs)


def propagate(field, hop_x, hop_y):
    inner = jnp.einsum("ax,nxy->nay", hop_x, field, precision=lax.Precision.HIGHEST)
    return jnp.einsum("nay,yb->nab", inner, hop_y, precision=lax.Precision.HIGHEST)


def normal_apply(vector, damp, hop_x, hop_y):
    num_devices = lax.axis_size("tm")
    position = lax.axis_index("tm")
    incoming = from_behind(vector, "tm", 1)
    incoming = incoming * jnp.where(position == 0, -1.0, 1.0).astype(jnp.float32)
    previous = jnp.concatenate([incoming, vector[:-1]], axis=0)
    forward = vector - propagate(damp * previous, hop_x, hop_y)
    carried = damp * propagate(forward, hop_x, hop_y)
    returning = from_behind(carried, "tm", -1)
    returning = returning * jnp.where(position == num_devices - 1, -1.0, 1.0).astype(jnp.float32)
    following = jnp.concatenate([carried[1:], returning], axis=0)
    return forward - following


def chebyshev(field, cosines, cbar, hop_x, hop_y):
    lower_edge = 0.05
    upper_edge = (1.0 + 3.0 * cbar) ** 2
    center = (upper_edge + lower_edge) / (upper_edge - lower_edge)
    radius_term = jnp.sqrt(center * center - 1.0)
    ratio = center - radius_term
    cos_block = cosines[:, None, None]

    def apply_shifted(vector):
        once = propagate(vector, hop_x, hop_y)
        twice = propagate(once, hop_x, hop_y)
        normal_part = vector + cbar * cbar * twice - 2.0 * cbar * cos_block * once
        return (2.0 * normal_part - (upper_edge + lower_edge) * vector) / (upper_edge - lower_edge)

    previous = field
    current = apply_shifted(field)
    weight = -ratio
    total_sum = previous + 2.0 * weight * current
    for degree in range(2, ORDER + 1):
        following = 2.0 * apply_shifted(current) - previous
        weight = weight * -ratio
        total_sum = total_sum + 2.0 * weight * following
        previous = current
        current = following
    return total_sum * (2.0 / ((upper_edge - lower_edge) * radius_term))


def precondition(resid, cbar, hop_x, hop_y):
    slices = resid.shape[0]
    side_x = resid.shape[1]
    side_y = resid.shape[2]
    num_devices = lax.axis_size("tm")
    length = slices * num_devices
    position = lax.axis_index("tm")
    flat = resid.reshape(slices, side_x * side_y)
    slab = lax.all_to_all(flat, "tm", split_axis=1, concat_axis=0, tiled=True)
    times = jnp.arange(length, dtype=jnp.int32)
    local_rows = position * slices + jnp.arange(slices, dtype=jnp.int32)
    freq_rows = times // 2
    phase = (2 * freq_rows[:, None] + 1) * times[None, :] % (2 * length)
    angles = phase.astype(jnp.float32) * (math.pi / length)
    basis_table = jnp.where((times % 2 == 0)[:, None], jnp.cos(angles), jnp.sin(angles))
    spectrum = jnp.dot(basis_table, slab, precision=lax.Precision.HIGHEST)
    components = lax.all_to_all(spectrum, "tm", split_axis=0, concat_axis=1, tiled=True)
    cosines = jnp.cos((2 * (local_rows // 2) + 1).astype(jnp.float32) * (math.pi / length))
    result = chebyshev(components.reshape(slices, side_x, side_y), cosines, cbar, hop_x, hop_y)
    returned = lax.all_to_all(
        result.reshape(slices, side_x * side_y), "tm", split_axis=1, concat_axis=0, tiled=True
    )
    back = jnp.dot(basis_table.T, returned, precision=lax.Precision.HIGHEST) * (2.0 / length)
    timeline = lax.all_to_all(back, "tm", split_axis=0, concat_axis=1, tiled=True)
    return timeline.reshape(slices, side_x, side_y)


def halves(value):
    high = value.astype(jnp.bfloat16)
    low = (value - high.astype(jnp.float32)).astype(jnp.bfloat16)
    return high, low


def left_stack(matrix):
    high, low = halves(matrix)
    return jnp.concatenate([high, high, low], axis=1)


def right_stack(matrix):
    high, low = halves(matrix)
    return jnp.concatenate([high, low, high], axis=0)


def product(left, right):
    return jnp.dot(left, right, preferred_element_type=jnp.float32)


def exact(left, right):
    return jnp.dot(left, right, precision=lax.Precision.HIGHEST, preferred_element_type=jnp.float32)


def fused_kernel(
    n, noise_ref, level_ref, hx_ref, hy_ref, tab_ref, cos_ref, sol_ref, res_ref,
    slab, spec, comp, zbuf, back, line, step, second, prev, carr, foll, vec, part, parts,
    left_ref, right_ref, hop_left, hop_right,
    a2a_send, a2a_recv, hop_send, hop_recv, sum_send, sum_recv,
):
    me = lax.axis_index("tm")
    side_x, side_y = hx_ref.shape[0], hy_ref.shape[0]
    rows = noise_ref.shape[1]
    whole = (side_x, side_y)
    blocks = (n, rows, side_y)

    barrier = pltpu.get_barrier_semaphore()

    def greet(i, carry):
        pl.semaphore_signal(
            barrier, inc=1, device_id={"tm": lax.rem(me + i, n)}, device_id_type=pl.DeviceIdType.MESH
        )
        return carry

    lax.fori_loop(1, n, greet, 0)
    pl.semaphore_wait(barrier, n - 1)

    def push(src, dst, send, recv, target):
        pltpu.make_async_remote_copy(
            src_ref=src, dst_ref=dst, send_sem=send, recv_sem=recv,
            device_id={"tm": target}, device_id_type=pl.DeviceIdType.MESH,
        ).start()

    def bytes_of(ref, sem):
        pltpu.make_async_copy(ref, ref, sem).wait()

    def scatter(src, dst, which):
        def one(i, carry):
            j = lax.rem(me + i, n)
            push(src.at[j], dst.at[me], a2a_send.at[which], a2a_recv.at[which], j)
            return carry

        lax.fori_loop(1, n, one, 0)
        dst[me] = src[me]

    def arrived(dst, which):
        bytes_of(dst.at[pl.ds(0, n - 1)], a2a_recv.at[which])

    def sent(src, which):
        bytes_of(src.at[pl.ds(0, n - 1)], a2a_send.at[which])

    def mix(source, j, entry):
        total = entry(j, 0) * source[0]
        for t in range(1, n):
            total = total + entry(j, t) * source[t]
        return total

    def mix_scatter(source, staged, dst, which, entry):
        def one(i, carry):
            j = lax.rem(me + i, n)
            staged[j] = mix(source, j, entry)
            push(staged.at[j], dst.at[me], a2a_send.at[which], a2a_recv.at[which], j)
            return carry

        lax.fori_loop(1, n, one, 0)
        dst[me] = mix(source, me, entry)

    forward_entry = lambda j, t: tab_ref[j, t]
    backward_entry = lambda j, t: tab_ref[t, j]

    scatter(noise_ref, slab.at[0], 0)

    levels = level_ref[...].astype(jnp.float32)
    middle = (LEVELS - 1) // 2
    folded = jnp.sum(levels.reshape(side_x // 8, 8, side_y), axis=0)
    lanes = part.shape[1]
    partial = folded[:, :lanes]
    for start in range(lanes, side_y, lanes):
        partial = partial + folded[:, start : start + lanes]
    part[...] = partial

    def share(i, carry):
        j = lax.rem(me + i, n)
        push(part, parts.at[me], sum_send, sum_recv, j)
        return carry

    lax.fori_loop(1, n, share, 0)
    parts[me] = part[...]

    hop_x = hx_ref[...]
    hop_y = hy_ref[...]
    hop_left[...] = left_stack(hop_x)
    hop_right[...] = right_stack(hop_y)
    left_ref[0:side_x] = hop_left[...]
    left_ref[side_x : 2 * side_x] = left_stack(exact(hop_x, hop_x))
    hop_y_twice = exact(hop_y, hop_y)
    damp = jnp.exp(-0.05 * (levels - middle))

    def propagate_one(field):
        inner = product(hop_left[...], right_of(field))
        return product(left_of(inner), hop_right[...])

    def right_of(field):
        high, low = halves(field)
        return jnp.concatenate([high, low, high], axis=0)

    def left_of(field):
        high, low = halves(field)
        return jnp.concatenate([high, high, low], axis=1)

    def chebyshev_local(field, consts):
        linear, weight0, ratio, scale = consts

        def doubled(vector):
            inner = product(left_ref[...], right_of(vector))
            both = jnp.concatenate([left_of(inner[:side_x]), left_of(inner[side_x:])], axis=1)
            return linear * vector + product(both, right_ref[...])

        current = 0.5 * doubled(field)
        total = field + 2.0 * weight0 * current

        def body(degree, carry):
            previous, current, total, weight = carry
            following = doubled(current) - previous
            weight = weight * weight0
            return current, following, total + 2.0 * weight * following, weight

        _, _, total, _ = lax.fori_loop(2, ORDER + 1, body, (field, current, total, weight0))
        return total * scale

    consts = None
    sign_first = jnp.where(me == 0, -1.0, 1.0).astype(jnp.float32)
    sign_last = jnp.where(me == n - 1, -1.0, 1.0).astype(jnp.float32)
    after = lax.rem(me + 1, n)
    before = lax.rem(me + n - 1, n)
    noise = noise_ref[...].reshape(whole)
    held = None
    for turn in range(2):
        at = 4 * turn
        source = noise_ref if turn == 0 else second
        arrived(slab.at[turn], at)
        mix_scatter(slab.at[turn], spec.at[turn], comp.at[turn], at + 1, forward_entry)
        if turn == 0:
            bytes_of(parts.at[pl.ds(0, n - 1)], sum_recv)
            level_sum = jnp.sum(jnp.sum(parts[...], axis=0), axis=(0, 1), keepdims=True)
            mean_level = level_sum / (n * side_x * side_y)
            cbar = jnp.exp(-0.05 * (mean_level - middle))
            lower = 0.05
            upper = (1.0 + 3.0 * cbar) * (1.0 + 3.0 * cbar)
            width = upper - lower
            center = (upper + lower) / width
            radius = jnp.sqrt(center * center - 1.0)
            ratio = center - radius
            linear = 2.0 * (2.0 - (upper + lower)) / width
            once = -8.0 * cbar * cos_ref[me] / width
            twice = 4.0 * cbar * cbar / width
            scale = (2.0 / (width * radius)) * (2.0 / n)
            right_ref[0 : 3 * side_y] = right_stack(once * hop_y)
            right_ref[3 * side_y : 6 * side_y] = right_stack(twice * hop_y_twice)
            consts = (linear, -ratio, ratio, scale)
        arrived(comp.at[turn], at + 1)
        zbuf[turn] = chebyshev_local(comp[turn].reshape(whole), consts).reshape(blocks)
        scatter(zbuf.at[turn], back.at[turn], at + 2)
        arrived(back.at[turn], at + 2)
        mix_scatter(back.at[turn], line.at[turn], step.at[turn], at + 3, backward_entry)
        arrived(step.at[turn], at + 3)
        vector = step[turn].reshape(whole)
        if turn == 1:
            vector = vec[0] + vector
            sol_ref[...] = vector.reshape(blocks)
        vec[turn] = vector
        push(vec.at[turn], prev.at[turn], hop_send.at[2 * turn], hop_recv.at[2 * turn], after)
        bytes_of(prev.at[turn], hop_recv.at[2 * turn])
        forward = vector - propagate_one(damp * (sign_first * prev[turn]))
        carr[turn] = damp * propagate_one(forward)
        push(carr.at[turn], foll.at[turn], hop_send.at[2 * turn + 1], hop_recv.at[2 * turn + 1], before)
        bytes_of(foll.at[turn], hop_recv.at[2 * turn + 1])
        rest = noise - (forward - sign_last * foll[turn])
        if turn == 0:
            second[...] = rest.reshape(blocks)
            scatter(second, slab.at[1], 4)
        else:
            res_ref[...] = rest.reshape(blocks)

    for turn in range(2):
        at = 4 * turn
        sent(noise_ref if turn == 0 else second, at)
        sent(spec.at[turn], at + 1)
        sent(zbuf.at[turn], at + 2)
        sent(line.at[turn], at + 3)
        bytes_of(vec.at[turn], hop_send.at[2 * turn])
        bytes_of(carr.at[turn], hop_send.at[2 * turn + 1])
    bytes_of(parts.at[pl.ds(0, n - 1)], sum_send)


def fused(noise, phonon_level, hop_x, hop_y):
    n = lax.axis_size("tm")
    side_x, side_y = noise.shape[1], noise.shape[2]
    rows = side_x // n
    blocks = (n, rows, side_y)
    times = jnp.arange(n, dtype=jnp.int32)
    freqs = times // 2
    phase = (2 * freqs[:, None] + 1) * times[None, :] % (2 * n)
    angles = phase.astype(jnp.float32) * (math.pi / n)
    table = jnp.where((times % 2 == 0)[:, None], jnp.cos(angles), jnp.sin(angles))
    cosines = jnp.cos((2 * freqs + 1).astype(jnp.float32) * (math.pi / n))
    f32, bf16 = jnp.float32, jnp.bfloat16
    pair = pltpu.VMEM((2,) + blocks, f32)
    plane = pltpu.VMEM((2, side_x, side_y), f32)
    vmem = pl.BlockSpec(memory_space=pltpu.VMEM)
    smem = pl.BlockSpec(memory_space=pltpu.SMEM)
    dma = pltpu.SemaphoreType.DMA
    out = jax.ShapeDtypeStruct(blocks, f32)
    sol, res = pl.pallas_call(
        functools.partial(fused_kernel, n),
        out_shape=(out, out),
        in_specs=[vmem] * 4 + [smem] * 2,
        out_specs=(vmem, vmem),
        scratch_shapes=[pair] * 7
        + [pltpu.VMEM(blocks, f32)]
        + [plane] * 4
        + [pltpu.VMEM((8, 128), f32), pltpu.VMEM((n, 8, 128), f32)]
        + [
            pltpu.VMEM((2 * side_x, 3 * side_x), bf16),
            pltpu.VMEM((6 * side_y, side_y), bf16),
            pltpu.VMEM((side_x, 3 * side_x), bf16),
            pltpu.VMEM((3 * side_y, side_y), bf16),
        ]
        + [dma((8,)), dma((8,)), dma((4,)), dma((4,)), dma(()), dma(())],
        compiler_params=pltpu.CompilerParams(
            collective_id=0, has_side_effects=True, vmem_limit_bytes=40 * 1024 * 1024
        ),
    )(noise.reshape(blocks), phonon_level.reshape(side_x, side_y), hop_x, hop_y, table, cosines)
    return sol.reshape(noise.shape), res.reshape(noise.shape)


def per_device(noise, phonon_level, hop_x, hop_y):
    slices = noise.shape[0]
    num_devices = lax.axis_size("tm")
    if slices == 1 and noise.shape[1] % (8 * num_devices) == 0 and noise.shape[2] % 128 == 0:
        return fused(noise, phonon_level, hop_x, hop_y)
    middle = (LEVELS - 1) // 2
    levels = phonon_level.astype(jnp.float32)
    damp = jnp.exp(-0.05 * (levels - middle))
    level_sum = lax.psum(jnp.sum(levels), "tm")
    mean_level = level_sum / (slices * num_devices * noise.shape[1] * noise.shape[2])
    cbar = jnp.exp(-0.05 * (mean_level - middle))
    first = precondition(noise, cbar, hop_x, hop_y)
    second_residual = noise - normal_apply(first, damp, hop_x, hop_y)
    solution = first + precondition(second_residual, cbar, hop_x, hop_y)
    residual = noise - normal_apply(solution, damp, hop_x, hop_y)
    return (solution, residual)


def solution(mesh):
    return jax.shard_map(
        per_device,
        mesh=mesh,
        in_specs=(P(("grp", "tm"), None, None), P(("grp", "tm"), None, None), P(), P()),
        out_specs=(P(("grp", "tm"), None, None), P(("grp", "tm"), None, None)),
        check_vma=False,
    )
```

```python
import functools
import math

import jax
import jax.numpy as jnp
from jax import lax
from jax.experimental import pallas as pl
from jax.experimental.pallas import tpu as pltpu
from jax.sharding import PartitionSpec as P

ORDER = 10
LEVELS = 17


def from_behind(value, axis, steps):
    count = lax.axis_size(axis)
    pairs = [(source, (source + steps) % count) for source in range(count)]
    return lax.ppermute(value, axis, pairs)


def propagate(field, hop_x, hop_y):
    inner = jnp.einsum("ax,nxy->nay", hop_x, field, precision=lax.Precision.HIGHEST)
    return jnp.einsum("nay,yb->nab", inner, hop_y, precision=lax.Precision.HIGHEST)


def normal_apply(vector, damp, hop_x, hop_y):
    num_devices = lax.axis_size("tm")
    position = lax.axis_index("tm")
    incoming = from_behind(vector, "tm", 1)
    incoming = incoming * jnp.where(position == 0, -1.0, 1.0).astype(jnp.float32)
    previous = jnp.concatenate([incoming, vector[:-1]], axis=0)
    forward = vector - propagate(damp * previous, hop_x, hop_y)
    carried = damp * propagate(forward, hop_x, hop_y)
    returning = from_behind(carried, "tm", -1)
    returning = returning * jnp.where(position == num_devices - 1, -1.0, 1.0).astype(jnp.float32)
    following = jnp.concatenate([carried[1:], returning], axis=0)
    return forward - following


def chebyshev(field, cosines, cbar, hop_x, hop_y):
    lower_edge = 0.05
    upper_edge = (1.0 + 3.0 * cbar) ** 2
    center = (upper_edge + lower_edge) / (upper_edge - lower_edge)
    radius_term = jnp.sqrt(center * center - 1.0)
    ratio = center - radius_term
    cos_block = cosines[:, None, None]

    def apply_shifted(vector):
        once = propagate(vector, hop_x, hop_y)
        twice = propagate(once, hop_x, hop_y)
        normal_part = vector + cbar * cbar * twice - 2.0 * cbar * cos_block * once
        return (2.0 * normal_part - (upper_edge + lower_edge) * vector) / (upper_edge - lower_edge)

    previous = field
    current = apply_shifted(field)
    weight = -ratio
    total_sum = previous + 2.0 * weight * current
    for degree in range(2, ORDER + 1):
        following = 2.0 * apply_shifted(current) - previous
        weight = weight * -ratio
        total_sum = total_sum + 2.0 * weight * following
        previous = current
        current = following
    return total_sum * (2.0 / ((upper_edge - lower_edge) * radius_term))


def precondition(resid, cbar, hop_x, hop_y):
    slices = resid.shape[0]
    side_x = resid.shape[1]
    side_y = resid.shape[2]
    num_devices = lax.axis_size("tm")
    length = slices * num_devices
    position = lax.axis_index("tm")
    flat = resid.reshape(slices, side_x * side_y)
    slab = lax.all_to_all(flat, "tm", split_axis=1, concat_axis=0, tiled=True)
    times = jnp.arange(length, dtype=jnp.int32)
    local_rows = position * slices + jnp.arange(slices, dtype=jnp.int32)
    freq_rows = times // 2
    phase = (2 * freq_rows[:, None] + 1) * times[None, :] % (2 * length)
    angles = phase.astype(jnp.float32) * (math.pi / length)
    basis_table = jnp.where((times % 2 == 0)[:, None], jnp.cos(angles), jnp.sin(angles))
    spectrum = jnp.dot(basis_table, slab, precision=lax.Precision.HIGHEST)
    components = lax.all_to_all(spectrum, "tm", split_axis=0, concat_axis=1, tiled=True)
    cosines = jnp.cos((2 * (local_rows // 2) + 1).astype(jnp.float32) * (math.pi / length))
    result = chebyshev(components.reshape(slices, side_x, side_y), cosines, cbar, hop_x, hop_y)
    returned = lax.all_to_all(
        result.reshape(slices, side_x * side_y), "tm", split_axis=1, concat_axis=0, tiled=True
    )
    back = jnp.dot(basis_table.T, returned, precision=lax.Precision.HIGHEST) * (2.0 / length)
    timeline = lax.all_to_all(back, "tm", split_axis=0, concat_axis=1, tiled=True)
    return timeline.reshape(slices, side_x, side_y)


def halves(value):
    high = value.astype(jnp.bfloat16)
    low = (value - high.astype(jnp.float32)).astype(jnp.bfloat16)
    return high, low


def left_stack(matrix):
    high, low = halves(matrix)
    return jnp.concatenate([high, high, low], axis=1)


def right_stack(matrix):
    high, low = halves(matrix)
    return jnp.concatenate([high, low, high], axis=0)


def product(left, right):
    return jnp.dot(left, right, preferred_element_type=jnp.float32)


def exact(left, right):
    return jnp.dot(left, right, precision=lax.Precision.HIGHEST, preferred_element_type=jnp.float32)


def fused_kernel(
    n, noise_ref, level_ref, hx_ref, hy_ref, tab_ref, cos_ref, sol_ref, res_ref,
    slab, spec, comp, zbuf, back, line, step, prev, carr, foll, vec,
    second, work, held, damp_ref, part, parts,
    left_ref, right_ref, hop_left, hop_right,
    a2a_send, a2a_recv, hop_send, hop_recv, sum_send, sum_recv,
):
    me = lax.axis_index("tm")
    side_x, side_y = hx_ref.shape[0], hy_ref.shape[0]
    rows = noise_ref.shape[1]
    whole = (side_x, side_y)
    blocks = (n, rows, side_y)
    chunks = rows // 8
    strip = (n, 8, side_y)
    flat = (8 * n, side_y)

    barrier = pltpu.get_barrier_semaphore()

    def greet(i, carry):
        pl.semaphore_signal(
            barrier, inc=1, device_id={"tm": lax.rem(me + i, n)}, device_id_type=pl.DeviceIdType.MESH
        )
        return carry

    lax.fori_loop(1, n, greet, 0)
    pl.semaphore_wait(barrier, n - 1)

    def push(src, dst, send, recv, target):
        pltpu.make_async_remote_copy(
            src_ref=src, dst_ref=dst, send_sem=send, recv_sem=recv,
            device_id={"tm": target}, device_id_type=pl.DeviceIdType.MESH,
        ).start()

    def bytes_of(ref, sem):
        pltpu.make_async_copy(ref, ref, sem).wait()

    def span(h):
        return pl.ds(8 * h, 8)

    def scatter(src, dst, which, h):
        def one(i, carry):
            j = lax.rem(me + i, n)
            push(
                src.at[j, span(h)], dst.at[me, span(h)],
                a2a_send.at[which], a2a_recv.at[which, h], j,
            )
            return carry

        lax.fori_loop(1, n, one, 0)
        dst[me, span(h)] = src[me, span(h)]

    def arrived(dst, which, h):
        bytes_of(dst.at[pl.ds(0, n - 1), span(h)], a2a_recv.at[which, h])

    def sent(src, which):
        bytes_of(src.at[pl.ds(0, n - 1)], a2a_send.at[which])

    def mix(source, j, entry, h):
        total = entry(j, 0) * source[0, span(h)]
        for t in range(1, n):
            total = total + entry(j, t) * source[t, span(h)]
        return total

    def mix_scatter(source, staged, dst, which, entry, h):
        def one(i, carry):
            j = lax.rem(me + i, n)
            staged[j, span(h)] = mix(source, j, entry, h)
            push(
                staged.at[j, span(h)], dst.at[me, span(h)],
                a2a_send.at[which], a2a_recv.at[which, h], j,
            )
            return carry

        lax.fori_loop(1, n, one, 0)
        dst[me, span(h)] = mix(source, me, entry, h)

    forward_entry = lambda j, t: tab_ref[j, t]
    backward_entry = lambda j, t: tab_ref[t, j]

    for h in range(chunks):
        scatter(noise_ref, slab.at[0], 0, h)

    levels = level_ref[...].astype(jnp.float32)
    middle = (LEVELS - 1) // 2
    folded = jnp.sum(levels.reshape(side_x // 8, 8, side_y), axis=0)
    lanes = part.shape[1]
    partial = folded[:, :lanes]
    for start in range(lanes, side_y, lanes):
        partial = partial + folded[:, start : start + lanes]
    part[...] = partial

    def share(i, carry):
        j = lax.rem(me + i, n)
        push(part, parts.at[me], sum_send, sum_recv, j)
        return carry

    lax.fori_loop(1, n, share, 0)
    parts[me] = part[...]

    hop_x = hx_ref[...]
    hop_y = hy_ref[...]
    hop_left[...] = left_stack(hop_x)
    hop_right[...] = right_stack(hop_y)
    left_ref[0:side_x] = hop_left[...]
    left_ref[side_x : 2 * side_x] = left_stack(exact(hop_x, hop_x))
    hop_y_twice = exact(hop_y, hop_y)
    damp_ref[...] = jnp.exp(-0.05 * (levels - middle)).reshape(blocks)

    def right_of(field):
        high, low = halves(field)
        return jnp.concatenate([high, low, high], axis=0)

    def left_of(field):
        high, low = halves(field)
        return jnp.concatenate([high, high, low], axis=1)

    def chebyshev_local(field, consts):
        linear, weight0, ratio, scale = consts

        def doubled(vector):
            inner = product(left_ref[...], right_of(vector))
            both = jnp.concatenate([left_of(inner[:side_x]), left_of(inner[side_x:])], axis=1)
            return linear * vector + product(both, right_ref[...])

        current = 0.5 * doubled(field)
        total = field + 2.0 * weight0 * current

        def body(degree, carry):
            previous, current, total, weight = carry
            following = doubled(current) - previous
            weight = weight * weight0
            return current, following, total + 2.0 * weight * following, weight

        _, _, total, _ = lax.fori_loop(2, ORDER + 1, body, (field, current, total, weight0))
        return total * scale

    consts = None
    sign_first = jnp.where(me == 0, -1.0, 1.0).astype(jnp.float32)
    sign_last = jnp.where(me == n - 1, -1.0, 1.0).astype(jnp.float32)
    after = lax.rem(me + 1, n)
    before = lax.rem(me + n - 1, n)
    for turn in range(2):
        at = 4 * turn
        for h in range(chunks):
            arrived(slab.at[turn], at, h)
            mix_scatter(slab.at[turn], spec.at[turn], comp.at[turn], at + 1, forward_entry, h)
        if turn == 0:
            bytes_of(parts.at[pl.ds(0, n - 1)], sum_recv)
            level_sum = jnp.sum(jnp.sum(parts[...], axis=0), axis=(0, 1), keepdims=True)
            mean_level = level_sum / (n * side_x * side_y)
            cbar = jnp.exp(-0.05 * (mean_level - middle))
            lower = 0.05
            upper = (1.0 + 3.0 * cbar) * (1.0 + 3.0 * cbar)
            width = upper - lower
            center = (upper + lower) / width
            radius = jnp.sqrt(center * center - 1.0)
            ratio = center - radius
            linear = 2.0 * (2.0 - (upper + lower)) / width
            once = -8.0 * cbar * cos_ref[me] / width
            twice = 4.0 * cbar * cbar / width
            scale = (2.0 / (width * radius)) * (2.0 / n)
            right_ref[0 : 3 * side_y] = right_stack(once * hop_y)
            right_ref[3 * side_y : 6 * side_y] = right_stack(twice * hop_y_twice)
            consts = (linear, -ratio, ratio, scale)
        for h in range(chunks):
            arrived(comp.at[turn], at + 1, h)
        zbuf[turn] = chebyshev_local(comp[turn].reshape(whole), consts).reshape(blocks)
        for h in range(chunks):
            scatter(zbuf.at[turn], back.at[turn], at + 2, h)
        for h in range(chunks):
            arrived(back.at[turn], at + 2, h)
            mix_scatter(back.at[turn], line.at[turn], step.at[turn], at + 3, backward_entry, h)
        for h in range(chunks):
            arrived(step.at[turn], at + 3, h)
            fresh = step[turn, :, span(h)]
            if turn == 1:
                fresh = vec[0, :, span(h)] + fresh
                sol_ref[:, span(h)] = fresh
            vec[turn, :, span(h)] = fresh
            push(
                vec.at[turn, :, span(h)], prev.at[turn, :, span(h)],
                hop_send.at[2 * turn], hop_recv.at[2 * turn, h], after,
            )
        for h in range(chunks):
            bytes_of(prev.at[turn, :, span(h)], hop_recv.at[2 * turn, h])
            damped = damp_ref[:, span(h)] * (sign_first * prev[turn, :, span(h)])
            work[:, span(h)] = product(left_of(damped.reshape(flat)), hop_right[...]).reshape(strip)
        hopped = product(hop_left[...], right_of(work[...].reshape(whole)))
        forward = vec[turn].reshape(whole) - hopped
        held[...] = forward.reshape(blocks)
        work[...] = product(hop_left[...], right_of(forward)).reshape(blocks)
        for h in range(chunks):
            inner = work[:, span(h)].reshape(flat)
            outer = product(left_of(inner), hop_right[...]).reshape(strip)
            carr[turn, :, span(h)] = damp_ref[:, span(h)] * outer
            push(
                carr.at[turn, :, span(h)], foll.at[turn, :, span(h)],
                hop_send.at[2 * turn + 1], hop_recv.at[2 * turn + 1, h], before,
            )
        for h in range(chunks):
            bytes_of(foll.at[turn, :, span(h)], hop_recv.at[2 * turn + 1, h])
            following = sign_last * foll[turn, :, span(h)]
            rest = noise_ref[:, span(h)] - (held[:, span(h)] - following)
            if turn == 0:
                second[:, span(h)] = rest
                scatter(second, slab.at[1], 4, h)
            else:
                res_ref[:, span(h)] = rest

    for turn in range(2):
        at = 4 * turn
        sent(noise_ref if turn == 0 else second, at)
        sent(spec.at[turn], at + 1)
        sent(zbuf.at[turn], at + 2)
        sent(line.at[turn], at + 3)
        bytes_of(vec.at[turn], hop_send.at[2 * turn])
        bytes_of(carr.at[turn], hop_send.at[2 * turn + 1])
    bytes_of(parts.at[pl.ds(0, n - 1)], sum_send)


def fused(noise, phonon_level, hop_x, hop_y):
    n = lax.axis_size("tm")
    side_x, side_y = noise.shape[1], noise.shape[2]
    rows = side_x // n
    blocks = (n, rows, side_y)
    times = jnp.arange(n, dtype=jnp.int32)
    freqs = times // 2
    phase = (2 * freqs[:, None] + 1) * times[None, :] % (2 * n)
    angles = phase.astype(jnp.float32) * (math.pi / n)
    table = jnp.where((times % 2 == 0)[:, None], jnp.cos(angles), jnp.sin(angles))
    cosines = jnp.cos((2 * freqs + 1).astype(jnp.float32) * (math.pi / n))
    f32, bf16 = jnp.float32, jnp.bfloat16
    pair = pltpu.VMEM((2,) + blocks, f32)
    chunks = rows // 8
    vmem = pl.BlockSpec(memory_space=pltpu.VMEM)
    smem = pl.BlockSpec(memory_space=pltpu.SMEM)
    dma = pltpu.SemaphoreType.DMA
    out = jax.ShapeDtypeStruct(blocks, f32)
    sol, res = pl.pallas_call(
        functools.partial(fused_kernel, n),
        out_shape=(out, out),
        in_specs=[vmem] * 4 + [smem] * 2,
        out_specs=(vmem, vmem),
        scratch_shapes=[pair] * 11
        + [pltpu.VMEM(blocks, f32)] * 4
        + [pltpu.VMEM((8, 128), f32), pltpu.VMEM((n, 8, 128), f32)]
        + [
            pltpu.VMEM((2 * side_x, 3 * side_x), bf16),
            pltpu.VMEM((6 * side_y, side_y), bf16),
            pltpu.VMEM((side_x, 3 * side_x), bf16),
            pltpu.VMEM((3 * side_y, side_y), bf16),
        ]
        + [dma((8,)), dma((8, chunks)), dma((4,)), dma((4, chunks)), dma(()), dma(())],
        compiler_params=pltpu.CompilerParams(
            collective_id=0, has_side_effects=True, vmem_limit_bytes=40 * 1024 * 1024
        ),
    )(noise.reshape(blocks), phonon_level.reshape(side_x, side_y), hop_x, hop_y, table, cosines)
    return sol.reshape(noise.shape), res.reshape(noise.shape)


def per_device(noise, phonon_level, hop_x, hop_y):
    slices = noise.shape[0]
    num_devices = lax.axis_size("tm")
    if slices == 1 and noise.shape[1] % (8 * num_devices) == 0 and noise.shape[2] % 128 == 0:
        return fused(noise, phonon_level, hop_x, hop_y)
    middle = (LEVELS - 1) // 2
    levels = phonon_level.astype(jnp.float32)
    damp = jnp.exp(-0.05 * (levels - middle))
    level_sum = lax.psum(jnp.sum(levels), "tm")
    mean_level = level_sum / (slices * num_devices * noise.shape[1] * noise.shape[2])
    cbar = jnp.exp(-0.05 * (mean_level - middle))
    first = precondition(noise, cbar, hop_x, hop_y)
    second_residual = noise - normal_apply(first, damp, hop_x, hop_y)
    solution = first + precondition(second_residual, cbar, hop_x, hop_y)
    residual = noise - normal_apply(solution, damp, hop_x, hop_y)
    return (solution, residual)


def solution(mesh):
    return jax.shard_map(
        per_device,
        mesh=mesh,
        in_specs=(P(("grp", "tm"), None, None), P(("grp", "tm"), None, None), P(), P()),
        out_specs=(P(("grp", "tm"), None, None), P(("grp", "tm"), None, None)),
        check_vma=False,
    )
```
